32 devices in a mesh: step: 4 (over z), band: 8 (over y, x, core).
Axes of the slice: x: 2, y: 2, z: 4, core: 2. Of those that a mesh axis runs over, the one named last changes fastest.
Arguments:
- states: float32 [4, 16, 10752], P('step', 'band'), may hold values from -6 to 6
- anchor: float32 [16, 10752], P('band'), may hold values from -6 to 6
- step_index: int32 [4], P('step'), may hold values from 0 to 19
- sigmas: float32 [20], replicated, may hold values from 0.05 to 0.5
- enc_w: bfloat16 [84, 512], replicated, may hold values from -0.625 to 0.625
- noise_embed: float32 [512], replicated, may hold values from -3 to 3
- qkv_w: bfloat16 [512, 1536], replicated, may hold values from -0.25 to 0.25
- out_w: bfloat16 [512, 512], replicated, may hold values from -0.25 to 0.25
- up_w: bfloat16 [512, 1024], replicated, may hold values from -0.25 to 0.25
- down_w: bfloat16 [1024, 512], replicated, may hold values from -0.1875 to 0.1875
- dec_w: bfloat16 [512, 84], replicated, may hold values from -0.25 to 0.25
Outputs:
- new_states: float32 [4, 16, 10752], P('step', 'band')
- change: float32 [4], P('step')
The draws below stay inside these ranges and needn't reach their ends.
All inputs are finite; a program needn't handle non-finite values.
Results may differ from the reference program's by a relative error of at most 0.0031.
Values may be sent and summed in bfloat16 or wider, within the bound.
A program may use at most 64 MiB of HBM per device.

```python
import math
import jax
import jax.numpy as jnp
from jax import lax

LAT_DEV = 2
LON = 128
C = 84
W = 512
HEADS = 4
HEAD_DIM = 128
MLP = 1024
LEVELS = 20
R = 2
STEPS = 4
NLAT = 16


def plant(result, stream_key, least, high):
    longest = result.shape.index(max(result.shape))
    spots = []
    for shift in (0, 1):
        where = [jax.random.randint(jax.random.fold_in(stream_key, axis), (), 0, length) for axis, length in enumerate(result.shape)]
        where[longest] = (where[longest] + shift) % result.shape[longest]
        spots.append(tuple(where))
    return result.at[spots[0]].set(least).at[spots[1]].set(high)


def block_scale(own_key, shape, split, smallest, largest):
    level, own = 1.0, jax.random.fold_in(own_key, 6)
    for dim, shards_of in split:
        heights = jnp.exp(jax.random.uniform(jax.random.fold_in(own, dim), (shards_of,), jnp.float32, smallest / len(split), largest / len(split)))
        level = level * jnp.repeat(heights, shape[dim] // shards_of).reshape([-1 if axis == dim else 1 for axis in range(len(shape))])
    return level


def bell_draw(rng, shape, width, bound, pieces=(), held_as=jnp.bfloat16):
    array = width * jax.random.normal(rng, shape, jnp.float32)
    if pieces:
        array = array * block_scale(rng, shape, pieces, -0.22, 0.18)
    return jnp.clip(array, -bound, bound).astype(held_as)


def setup_inputs(seed: int = 0) -> dict:
    keys = jax.random.split(jax.random.key(seed), 12)
    states = bell_draw(keys[0], (STEPS, NLAT, LON * C), 1.0, 6.0, ((0, 4), (1, 8)), jnp.float32)
    anchor = bell_draw(keys[1], (NLAT, LON * C), 1.0, 6.0, ((0, 8),), jnp.float32)
    step_index = plant(jax.random.randint(keys[2], (STEPS,), 0, LEVELS), jax.random.fold_in(keys[2], 1), 0, LEVELS - 1).astype(jnp.int32)
    sigmas = jnp.clip(jnp.exp(jax.random.uniform(keys[3], (LEVELS,), jnp.float32, math.log(0.05), math.log(0.5))), 0.05, 0.5)
    enc_w = bell_draw(keys[4], (C, W), C ** -0.5, 0.625)
    noise_embed = bell_draw(keys[5], (W,), 0.5, 3.0, (), jnp.float32)
    qkv_w = bell_draw(keys[6], (W, 3 * W), W ** -0.5, 0.25)
    out_w = bell_draw(keys[7], (W, W), W ** -0.5, 0.25)
    up_w = bell_draw(keys[8], (W, MLP), W ** -0.5, 0.25)
    down_w = bell_draw(keys[9], (MLP, W), MLP ** -0.5, 0.1875)
    dec_w = bell_draw(keys[10], (W, C), W ** -0.5, 0.25)
    return {"states": states, "anchor": anchor, "step_index": step_index, "sigmas": sigmas, "enc_w": enc_w, "noise_embed": noise_embed, "qkv_w": qkv_w, "out_w": out_w, "up_w": up_w, "down_w": down_w, "dec_w": dec_w}


epsilon = 1e-06
score_gain = 3.0

def rms_scale(values):
    return values * lax.rsqrt(lax.optimization_barrier(jnp.mean(values * values, axis=-1, keepdims=True)) + epsilon)

def split_heads(projected):
    heads = rms_scale(projected.reshape(projected.shape[0], HEADS, HEAD_DIM))
    return heads.astype(jnp.bfloat16)

def window_mask_for(first_row, lat_rows, total_rows):
    offsets = jnp.arange(lat_rows + 2 * R, dtype=jnp.int32) - R
    key_rows = first_row + offsets
    inside = (key_rows >= 0) & (key_rows < total_rows)
    near = jnp.abs(jnp.arange(lat_rows, dtype=jnp.int32)[:, None] - offsets[None, :]) <= R
    return (inside[None, :] & near).astype(jnp.float32)

def attend(queries, key_heads, value_heads, window_mask):
    scores = jnp.einsum('qhd,khd->hqk', queries.astype(jnp.float32), key_heads.astype(jnp.float32))
    scores = scores * (score_gain / math.sqrt(HEAD_DIM))
    heads, count_q, count_k = scores.shape
    rows_q = window_mask.shape[0]
    rows_k = window_mask.shape[1]
    columns = count_q // rows_q
    weights = jnp.exp(scores).reshape(heads, rows_q, columns, rows_k, columns)
    weights = (weights * window_mask[None, :, None, :, None]).reshape(heads, count_q, count_k)
    softmax_weights = (weights / lax.optimization_barrier(jnp.sum(weights, axis=-1, keepdims=True))).astype(jnp.bfloat16)
    attended = jnp.einsum('hqk,khd->qhd', softmax_weights.astype(jnp.float32), value_heads.astype(jnp.float32))
    return attended.astype(jnp.bfloat16).reshape(count_q, W)

def finish_block(embedded, attended, out_w, up_w, down_w, dec_w):
    mixed = embedded + jnp.dot(attended, out_w, preferred_element_type=jnp.float32)
    normed = rms_scale(mixed).astype(jnp.bfloat16)
    hidden = jax.nn.gelu(jnp.dot(normed, up_w, preferred_element_type=jnp.float32)).astype(jnp.bfloat16)
    mixed = mixed + jnp.dot(hidden, down_w, preferred_element_type=jnp.float32)
    return jnp.dot(rms_scale(mixed).astype(jnp.bfloat16), dec_w, preferred_element_type=jnp.float32)

def step_drift(fields, noise_level, enc_w, noise_embed, qkv_w, out_w, up_w, down_w, dec_w):
    columns = fields.shape[1] // C
    tokens = fields.astype(jnp.bfloat16).reshape(-1, C)
    embedded = jnp.dot(tokens, enc_w, preferred_element_type=jnp.float32) + (jnp.log(noise_level) * noise_embed)[None, :]
    normed = rms_scale(embedded).astype(jnp.bfloat16)
    projected = jnp.dot(normed, qkv_w, preferred_element_type=jnp.float32)
    queries = split_heads(projected[:, :W]).reshape(NLAT, columns, HEADS, HEAD_DIM)
    key_heads = split_heads(projected[:, W:2 * W]).reshape(NLAT, columns, HEADS, HEAD_DIM)
    value_heads = projected[:, 2 * W:].astype(jnp.bfloat16).reshape(NLAT, columns, HEADS, HEAD_DIM)
    padding = ((R, R), (0, 0), (0, 0), (0, 0))
    key_grid = jnp.pad(key_heads, padding)
    value_grid = jnp.pad(value_heads, padding)
    embed_grid = embedded.reshape(NLAT, columns, W)

    def one_band(band):
        first_row = (band * LAT_DEV).astype(jnp.int32)
        band_queries = lax.dynamic_slice_in_dim(queries, first_row, LAT_DEV, 0).reshape(-1, HEADS, HEAD_DIM)
        band_keys = lax.dynamic_slice_in_dim(key_grid, first_row, LAT_DEV + 2 * R, 0).reshape(-1, HEADS, HEAD_DIM)
        band_values = lax.dynamic_slice_in_dim(value_grid, first_row, LAT_DEV + 2 * R, 0).reshape(-1, HEADS, HEAD_DIM)
        band_embed = lax.dynamic_slice_in_dim(embed_grid, first_row, LAT_DEV, 0).reshape(-1, W)
        window_mask = window_mask_for(first_row, LAT_DEV, NLAT)
        attended = attend(band_queries, band_keys, band_values, window_mask)
        drift_rows = finish_block(band_embed, attended, out_w, up_w, down_w, dec_w)
        return drift_rows.reshape(LAT_DEV, columns * C)
    drifts = lax.map(one_band, jnp.arange(NLAT // LAT_DEV, dtype=jnp.int32))
    return drifts.reshape(NLAT, columns * C)

def reference(states, anchor, step_index, sigmas, enc_w, noise_embed, qkv_w, out_w, up_w, down_w, dec_w):
    inputs = jnp.concatenate([anchor[None], states[:-1]], axis=0)
    noise_levels = sigmas[step_index]

    def one_step(packed):
        fields, noise_level = packed
        return step_drift(fields, noise_level, enc_w, noise_embed, qkv_w, out_w, up_w, down_w, dec_w)
    drifts = lax.map(one_step, (inputs, noise_levels))
    new_states = anchor[None] + jnp.cumsum(noise_levels[:, None, None] * drifts, axis=0)
    latitude = jnp.pi * ((jnp.arange(NLAT, dtype=jnp.float32) + 0.5) / NLAT - 0.5)
    area = jnp.cos(latitude)
    mismatch = new_states - states
    change = lax.optimization_barrier(jnp.sum(area[None, :, None] * mismatch * mismatch, axis=(1, 2))) / (jnp.sum(area) * (LON * C))
    return (new_states, change)
```

```python
import functools
import math

import jax
import jax.numpy as jnp
import numpy as np
from jax import lax
from jax.experimental import pallas as pl
from jax.experimental.pallas import tpu as pltpu
from jax.sharding import PartitionSpec as P

HEADS = 4
R = 2
LANES = 128
CHUNKS = 3

epsilon = 1e-06
score_gain = 3.0

MESH = pl.DeviceIdType.MESH


def rms_scale(values):
    return values * lax.rsqrt(jnp.mean(values * values, axis=-1, keepdims=True) + epsilon)


def dot(a, b):
    return jnp.dot(a, b, preferred_element_type=jnp.float32)


def kernel(
    sizes,
    step_index, sigmas, states_hbm, anchor_hbm, enc_hbm, embed_hbm, qkv_hbm, out_hbm, up_hbm,
    down_hbm, dec_hbm,
    new_ref, change_ref,
    states_flat, anchor_flat, enc_w, noise_embed, qkv_w, out_w, up_w, down_w, dec_w,
    states_rows, anchor_rows, sent, fields, keys, values, attended, padded,
    carry_in, carry_out, partials, load_sem, sent_sem, fields_sem, carry_send, carry_recv,
    part_send, part_recv,
):
    steps, bands = sizes
    step, band = lax.axis_index("step"), lax.axis_index("band")
    lat_rows, width = states_flat.shape
    channels, model = enc_w.shape
    columns = width // channels
    tokens = lat_rows * columns
    groups = width // LANES
    rows = states_rows.shape[0]
    padded_rows = sent.shape[0]
    head = model // HEADS
    above, below = band > 0, band < bands - 1
    opens, closes = step == 0, step == steps - 1

    pairs = (
        (states_hbm.at[0], states_flat), (anchor_hbm, anchor_flat), (enc_hbm, enc_w),
        (embed_hbm, noise_embed), (qkv_hbm, qkv_w), (out_hbm, out_w), (up_hbm, up_w),
        (down_hbm, down_w), (dec_hbm, dec_w),
    )
    loads = [pltpu.make_async_copy(a, b, load_sem.at[i]) for i, (a, b) in enumerate(pairs)]
    for load in loads:
        load.start()

    barrier = pltpu.get_barrier_semaphore()

    def greet(to_step, to_band):
        pl.semaphore_signal(barrier, inc=1, device_id=(to_step, to_band), device_id_type=MESH)

    @pl.when(step > 0)
    def _():
        greet(step - 1, band)

        @pl.when(above)
        def _():
            greet(step - 1, band - 1)

        @pl.when(below)
        def _():
            greet(step - 1, band + 1)

    for d in range(1, bands):
        greet(step, lax.rem(band + d, bands))

    def to_rows(flat, out):
        for g in range(groups):
            out[lat_rows * g : lat_rows * (g + 1), :] = flat[:, LANES * g : LANES * (g + 1)]

    loads[0].wait()
    to_rows(states_flat, states_rows)
    zero_rows = jnp.zeros((padded_rows - rows, LANES), jnp.float32)
    sent[...] = jnp.concatenate([states_rows[...], zero_rows], axis=0).astype(jnp.bfloat16)
    loads[1].wait()
    to_rows(anchor_flat, anchor_rows)

    @pl.when(opens)
    def _():
        fields[1] = jnp.concatenate([anchor_rows[...], zero_rows], axis=0).astype(jnp.bfloat16)

    onward = 1 + above.astype(jnp.int32) + below.astype(jnp.int32)
    pl.semaphore_wait(barrier, bands - 1 + jnp.where(closes, 0, onward))

    def field_copy(source, slot, sem, to_step, to_band):
        return pltpu.make_async_remote_copy(
            src_ref=source, dst_ref=fields.at[slot], send_sem=sent_sem.at[sem],
            recv_sem=fields_sem.at[slot], device_id=(to_step, to_band), device_id_type=MESH,
        )

    to_center = field_copy(sent, 1, 0, step + 1, band)
    to_above = field_copy(sent, 2, 1, step + 1, band - 1)
    to_below = field_copy(sent, 0, 2, step + 1, band + 1)
    open_above = field_copy(fields.at[1], 2, 3, step, band - 1)
    open_below = field_copy(fields.at[1], 0, 4, step, band + 1)

    def for_fields(act):
        @pl.when(jnp.logical_not(closes))
        def _():
            act(to_center)

            @pl.when(above)
            def _():
                act(to_above)

            @pl.when(below)
            def _():
                act(to_below)

        @pl.when(opens)
        def _():
            @pl.when(above)
            def _():
                act(open_above)

            @pl.when(below)
            def _():
                act(open_below)

    for_fields(lambda copy: copy.start())

    @pl.when(jnp.logical_not(above))
    def _():
        fields[0] = jnp.zeros((padded_rows, LANES), jnp.bfloat16)

    @pl.when(jnp.logical_not(below))
    def _():
        fields[2] = jnp.zeros((padded_rows, LANES), jnp.bfloat16)

    unit = math.gcd(channels, LANES)
    period = LANES // unit
    stride = pow(-(channels // unit), -1, period)

    def column_of(token):
        place, turn = token % columns, token % period
        return place - turn + (turn * stride) % period

    def places(shape, token_dim, row_dim, later):
        token = lax.broadcasted_iota(jnp.int32, shape, token_dim)
        row = lax.broadcasted_iota(jnp.int32, shape, row_dim)
        lat, column = token // columns, column_of(token)
        first = (column * channels) // LANES + later
        return (row == first * lat_rows + lat).astype(jnp.float32).astype(jnp.bfloat16)

    gather_first = places((tokens, padded_rows), 0, 1, 0)
    gather_next = places((tokens, padded_rows), 0, 1, 1)
    token = lax.broadcasted_iota(jnp.int32, (tokens, LANES), 0)
    lane = lax.broadcasted_iota(jnp.int32, (tokens, LANES), 1)
    in_first = lane >= (column_of(token) * channels) % LANES

    noise = sigmas[step_index[0]]
    loads[2].wait()
    loads[3].wait()
    offset = jnp.log(jnp.full((1, model), noise, jnp.float32)) * noise_embed[...].reshape(1, model)
    loads[4].wait()

    def embed(slot):
        packed = fields[slot]
        picked = jnp.where(in_first, dot(gather_first, packed), dot(gather_next, packed))
        turned = pltpu.roll(picked, 0, 1, stride=unit, stride_axis=0)
        return dot(turned[:, :channels].astype(jnp.bfloat16), enc_w[...]) + offset

    def keep_key_value(slot, key_value, valid):
        at = slice(slot * tokens, (slot + 1) * tokens)
        for h in range(HEADS):
            here = slice(h * head, (h + 1) * head)
            keys[at, here] = rms_scale(key_value[:, here]).astype(jnp.bfloat16)
            value = key_value[:, model + h * head : model + (h + 1) * head]
            ones = jnp.ones((tokens, head), jnp.float32)
            if valid is not None:
                value, ones = value * valid, ones * valid
            values[at, 2 * h * head : (2 * h + 1) * head] = value.astype(jnp.bfloat16)
            values[at, (2 * h + 1) * head : (2 * h + 2) * head] = ones.astype(jnp.bfloat16)

    @pl.when(jnp.logical_not(opens))
    def _():
        to_center.wait_recv()

    embedded = embed(1)
    projected = dot(rms_scale(embedded).astype(jnp.bfloat16), qkv_w[...])
    queries = [
        rms_scale(projected[:, h * head : (h + 1) * head]).astype(jnp.bfloat16)
        for h in range(HEADS)
    ]
    keep_key_value(1, projected[:, model:], None)

    for slot, there, copy in ((0, above, to_below), (2, below, to_above)):
        pl.when(there)(copy.wait_recv)
        normed = rms_scale(embed(slot)).astype(jnp.bfloat16)
        keep_key_value(slot, dot(normed, qkv_w[:, model:]), there.astype(jnp.float32))

    gain = score_gain / math.sqrt(head) * math.log2(math.e)
    for h in range(HEADS):
        for i in range(lat_rows):
            window = slice(i * columns, (i + 2 * R + 1) * columns)
            mine = slice(i * columns, (i + 1) * columns)
            scores = lax.dot_general(
                queries[h][mine], keys[window, h * head : (h + 1) * head],
                (((1,), (1,)), ((), ())), preferred_element_type=jnp.float32,
            )
            weights = jnp.exp2(scores * gain).astype(jnp.bfloat16)
            sums = dot(weights, values[window, 2 * h * head : (2 * h + 2) * head])
            attended[mine, h * head : (h + 1) * head] = (
                sums[:, :head] / sums[:, head:]
            ).astype(jnp.bfloat16)

    loads[5].wait()
    mixed = embedded + dot(attended[...], out_w[...])
    loads[6].wait()
    hidden = jax.nn.gelu(dot(rms_scale(mixed).astype(jnp.bfloat16), up_w[...]))
    loads[7].wait()
    mixed = mixed + dot(hidden.astype(jnp.bfloat16), down_w[...])
    loads[8].wait()
    padded[...] = jnp.zeros_like(padded)
    padded[:, :channels] = lax.dot_general(
        rms_scale(mixed).astype(jnp.bfloat16), dec_w[...], (((1,), (1,)), ((), ())),
        preferred_element_type=jnp.float32,
    )

    turned = padded[...]
    turns = (period - token % period) % period
    for bit in range((period - 1).bit_length()):
        turned = jnp.where((turns >> bit) % 2 == 1, pltpu.roll(turned, unit << bit, 1), turned)
    split = jnp.concatenate(
        [jnp.where(in_first, turned, 0.0), jnp.where(in_first, 0.0, turned)], axis=0
    )
    coarse = split.astype(jnp.bfloat16)
    fine = (split - coarse.astype(jnp.float32)).astype(jnp.bfloat16)
    scatter = jnp.concatenate(
        [places((padded_rows, tokens), 1, 0, 0), places((padded_rows, tokens), 1, 0, 1)], axis=1
    )
    both = dot(scatter, jnp.concatenate([coarse, fine], axis=1))
    own = noise * (both[:rows, :LANES] + both[:rows, LANES:])

    piece = rows // CHUNKS
    carries = []
    for c in range(CHUNKS):
        at = slice(c * piece, (c + 1) * piece)
        carries.append(
            pltpu.make_async_remote_copy(
                src_ref=carry_out.at[at], dst_ref=carry_in.at[at], send_sem=carry_send.at[c],
                recv_sem=carry_recv.at[c], device_id=(step + 1, band), device_id_type=MESH,
            )
        )

    @pl.when(opens)
    def _():
        carry_in[...] = jnp.zeros_like(carry_in)

    partial = jnp.zeros((8, LANES), jnp.float32)
    for c, carry in enumerate(carries):
        at = slice(c * piece, (c + 1) * piece)
        pl.when(jnp.logical_not(opens))(carry.wait_recv)
        carry_out[at] = carry_in[at] + own[at]
        pl.when(jnp.logical_not(closes))(carry.start)
        renewed = anchor_rows[at] + carry_out[at]
        mismatch = renewed - states_rows[at]
        partial += jnp.sum((mismatch * mismatch).reshape(piece // 8, 8, LANES), axis=0)
        for g in range(c * piece // lat_rows, (c + 1) * piece // lat_rows):
            low = lat_rows * g - c * piece
            new_ref[0, :, LANES * g : LANES * (g + 1)] = renewed[low : low + lat_rows]

    total_rows = lat_rows * bands
    table = np.cos(np.pi * ((np.arange(total_rows) + 0.5) / total_rows - 0.5))
    lat = lax.broadcasted_iota(jnp.int32, (8, LANES), 0) % lat_rows + band * lat_rows
    area = jnp.zeros((8, LANES), jnp.float32)
    for i, value in enumerate(table):
        area = jnp.where(lat == i, float(value), area)
    partials[band] = partial * area

    parts = [
        pltpu.make_async_remote_copy(
            src_ref=partials.at[band], dst_ref=partials.at[band], send_sem=part_send.at[d - 1],
            recv_sem=part_recv.at[d - 1], device_id=(step, lax.rem(band + d, bands)),
            device_id_type=MESH,
        )
        for d in range(1, bands)
    ]
    for part in parts:
        part.start()
    for part in parts:
        part.wait_recv()
    total = jnp.sum(partials[...], axis=0)
    change_ref[0] = jnp.sum(total) * (1.0 / float(np.sum(table) * width))

    for part in parts:
        part.wait_send()
    for carry in carries:
        pl.when(jnp.logical_not(closes))(carry.wait_send)
    for_fields(lambda copy: copy.wait_send())


def local(
    sizes, states, anchor, step_index, sigmas, enc_w, noise_embed, qkv_w, out_w, up_w, down_w, dec_w
):
    _, lat_rows, width = states.shape
    channels, model = enc_w.shape
    columns = width // channels
    rows = lat_rows * width // LANES
    padded_rows = -(-rows // 16) * 16
    tokens = lat_rows * columns
    steps, bands = sizes
    f32, bf16 = jnp.float32, jnp.bfloat16
    weights = (enc_w, noise_embed, qkv_w, out_w, up_w, down_w, dec_w.T)
    hbm = pl.BlockSpec(memory_space=pl.ANY)
    smem = pl.BlockSpec(memory_space=pltpu.SMEM)
    dma = pltpu.SemaphoreType.DMA
    return pl.pallas_call(
        functools.partial(kernel, sizes),
        out_shape=(
            jax.ShapeDtypeStruct(states.shape, f32),
            jax.ShapeDtypeStruct((1,), f32),
        ),
        in_specs=[smem, smem] + [hbm] * 9,
        out_specs=(pl.BlockSpec(memory_space=pltpu.VMEM), smem),
        scratch_shapes=[
            pltpu.VMEM((lat_rows, width), f32),
            pltpu.VMEM((lat_rows, width), f32),
        ]
        + [pltpu.VMEM(w.shape, w.dtype) for w in weights]
        + [
            pltpu.VMEM((rows, LANES), f32),
            pltpu.VMEM((rows, LANES), f32),
            pltpu.VMEM((padded_rows, LANES), bf16),
            pltpu.VMEM((3, padded_rows, LANES), bf16),
            pltpu.VMEM((3 * tokens, model), bf16),
            pltpu.VMEM((3 * tokens, 2 * model), bf16),
            pltpu.VMEM((tokens, model), bf16),
            pltpu.VMEM((tokens, LANES), f32),
            pltpu.VMEM((rows, LANES), f32),
            pltpu.VMEM((rows, LANES), f32),
            pltpu.VMEM((bands, 8, LANES), f32),
            dma((9,)),
            dma((5,)),
            dma((3,)),
            dma((CHUNKS,)),
            dma((CHUNKS,)),
            dma((bands - 1,)),
            dma((bands - 1,)),
        ],
        compiler_params=pltpu.CompilerParams(
            collective_id=0, has_side_effects=True, vmem_limit_bytes=48 * 1024 * 1024
        ),
        cost_estimate=pl.CostEstimate(flops=2 * 10**9, bytes_accessed=5 * 10**6, transcendentals=10**6),
    )(step_index, sigmas, states, anchor, *weights)


def solution(mesh):
    placed = (
        P("step", "band", None), P("band", None), P("step"),
        P(), P(), P(), P(), P(), P(), P(), P(),
    )
    return jax.shard_map(
        functools.partial(local, (mesh.shape["step"], mesh.shape["band"])),
        mesh=mesh,
        in_specs=placed,
        out_specs=(P("step", "band", None), P("step")),
        check_vma=False,
    )
```

```python
import functools
import math

import jax
import jax.numpy as jnp
import numpy as np
from jax import lax
from jax.experimental import pallas as pl
from jax.experimental.pallas import tpu as pltpu
from jax.sharding import PartitionSpec as P

HEADS = 4
R = 2
LANES = 128
CHUNKS = 7

epsilon = 1e-06
score_gain = 3.0

MESH = pl.DeviceIdType.MESH


def rms_scale(values):
    return values * lax.rsqrt(jnp.mean(values * values, axis=-1, keepdims=True) + epsilon)


def dot(a, b):
    return jnp.dot(a, b, preferred_element_type=jnp.float32)


def kernel(
    sizes,
    step_index, sigmas, states_hbm, anchor_hbm, enc_hbm, embed_hbm, qkv_hbm, out_hbm, up_hbm,
    down_hbm, dec_hbm,
    new_ref, change_ref,
    states_flat, anchor_flat, enc_w, noise_embed, qkv_w, out_w, up_w, down_w, dec_w,
    states_rows, anchor_rows, sent, fields, keys, values, attended, padded,
    carry_in, carry_out, partials, load_sem, sent_sem, fields_sem, carry_send, carry_recv,
    part_send, part_recv,
):
    steps, bands = sizes
    step, band = lax.axis_index("step"), lax.axis_index("band")
    lat_rows, width = states_flat.shape
    channels, model = enc_w.shape
    columns = width // channels
    tokens = lat_rows * columns
    groups = width // LANES
    rows = states_rows.shape[0]
    padded_rows = sent.shape[0]
    head = model // HEADS
    above, below = band > 0, band < bands - 1
    opens, closes = step == 0, step == steps - 1

    pairs = (
        (states_hbm.at[0], states_flat), (anchor_hbm, anchor_flat), (enc_hbm, enc_w),
        (embed_hbm, noise_embed), (qkv_hbm, qkv_w), (out_hbm, out_w), (up_hbm, up_w),
        (down_hbm, down_w), (dec_hbm, dec_w),
    )
    loads = [pltpu.make_async_copy(a, b, load_sem.at[i]) for i, (a, b) in enumerate(pairs)]
    for load in loads:
        load.start()

    barrier = pltpu.get_barrier_semaphore()

    def greet(to_step, to_band):
        pl.semaphore_signal(barrier, inc=1, device_id=(to_step, to_band), device_id_type=MESH)

    @pl.when(step > 0)
    def _():
        greet(step - 1, band)

        @pl.when(above)
        def _():
            greet(step - 1, band - 1)

        @pl.when(below)
        def _():
            greet(step - 1, band + 1)

    for d in range(1, bands):
        greet(step, lax.rem(band + d, bands))

    def to_rows(flat, out):
        for g in range(groups):
            out[lat_rows * g : lat_rows * (g + 1), :] = flat[:, LANES * g : LANES * (g + 1)]

    loads[0].wait()
    to_rows(states_flat, states_rows)
    zero_rows = jnp.zeros((padded_rows - rows, LANES), jnp.float32)
    sent[...] = jnp.concatenate([states_rows[...], zero_rows], axis=0).astype(jnp.bfloat16)
    loads[1].wait()
    to_rows(anchor_flat, anchor_rows)

    @pl.when(opens)
    def _():
        fields[1] = jnp.concatenate([anchor_rows[...], zero_rows], axis=0).astype(jnp.bfloat16)

    onward = 1 + above.astype(jnp.int32) + below.astype(jnp.int32)
    pl.semaphore_wait(barrier, bands - 1 + jnp.where(closes, 0, onward))

    def field_copy(source, slot, sem, to_step, to_band):
        return pltpu.make_async_remote_copy(
            src_ref=source, dst_ref=fields.at[slot], send_sem=sent_sem.at[sem],
            recv_sem=fields_sem.at[slot], device_id=(to_step, to_band), device_id_type=MESH,
        )

    to_center = field_copy(sent, 1, 0, step + 1, band)
    to_above = field_copy(sent, 2, 1, step + 1, band - 1)
    to_below = field_copy(sent, 0, 2, step + 1, band + 1)
    open_above = field_copy(fields.at[1], 2, 3, step, band - 1)
    open_below = field_copy(fields.at[1], 0, 4, step, band + 1)

    def for_fields(act):
        @pl.when(jnp.logical_not(closes))
        def _():
            act(to_center)

            @pl.when(above)
            def _():
                act(to_above)

            @pl.when(below)
            def _():
                act(to_below)

        @pl.when(opens)
        def _():
            @pl.when(above)
            def _():
                act(open_above)

            @pl.when(below)
            def _():
                act(open_below)

    for_fields(lambda copy: copy.start())

    @pl.when(jnp.logical_not(above))
    def _():
        fields[0] = jnp.zeros((padded_rows, LANES), jnp.bfloat16)

    @pl.when(jnp.logical_not(below))
    def _():
        fields[2] = jnp.zeros((padded_rows, LANES), jnp.bfloat16)

    unit = math.gcd(channels, LANES)
    period = LANES // unit
    stride = pow(-(channels // unit), -1, period)

    def column_of(token):
        place, turn = token % columns, token % period
        return place - turn + (turn * stride) % period

    def places(shape, token_dim, row_dim, later):
        token = lax.broadcasted_iota(jnp.int32, shape, token_dim)
        row = lax.broadcasted_iota(jnp.int32, shape, row_dim)
        lat, column = token // columns, column_of(token)
        first = (column * channels) // LANES + later
        return (row == first * lat_rows + lat).astype(jnp.float32).astype(jnp.bfloat16)

    gather_first = places((tokens, padded_rows), 0, 1, 0)
    gather_next = places((tokens, padded_rows), 0, 1, 1)
    token = lax.broadcasted_iota(jnp.int32, (tokens, LANES), 0)
    lane = lax.broadcasted_iota(jnp.int32, (tokens, LANES), 1)
    in_first = lane >= (column_of(token) * channels) % LANES

    noise = sigmas[step_index[0]]
    loads[2].wait()
    loads[3].wait()
    offset = jnp.log(jnp.full((1, model), noise, jnp.float32)) * noise_embed[...].reshape(1, model)
    loads[4].wait()

    def embed(slot):
        packed = fields[slot]
        picked = jnp.where(in_first, dot(gather_first, packed), dot(gather_next, packed))
        turned = pltpu.roll(picked, 0, 1, stride=unit, stride_axis=0)
        return dot(turned[:, :channels].astype(jnp.bfloat16), enc_w[...]) + offset

    def keep_key_value(slot, key_value, valid):
        at = slice(slot * tokens, (slot + 1) * tokens)
        for h in range(HEADS):
            here = slice(h * head, (h + 1) * head)
            keys[at, here] = rms_scale(key_value[:, here]).astype(jnp.bfloat16)
            value = key_value[:, model + h * head : model + (h + 1) * head]
            ones = jnp.ones((tokens, head), jnp.float32)
            if valid is not None:
                value, ones = value * valid, ones * valid
            values[at, 2 * h * head : (2 * h + 1) * head] = value.astype(jnp.bfloat16)
            values[at, (2 * h + 1) * head : (2 * h + 2) * head] = ones.astype(jnp.bfloat16)

    @pl.when(jnp.logical_not(opens))
    def _():
        to_center.wait_recv()

    embedded = embed(1)
    projected = dot(rms_scale(embedded).astype(jnp.bfloat16), qkv_w[...])
    queries = [
        rms_scale(projected[:, h * head : (h + 1) * head]).astype(jnp.bfloat16)
        for h in range(HEADS)
    ]
    keep_key_value(1, projected[:, model:], None)

    for slot, there, copy in ((0, above, to_below), (2, below, to_above)):
        pl.when(there)(copy.wait_recv)
        normed = rms_scale(embed(slot)).astype(jnp.bfloat16)
        keep_key_value(slot, dot(normed, qkv_w[:, model:]), there.astype(jnp.float32))

    gain = score_gain / math.sqrt(head) * math.log2(math.e)
    for h in range(HEADS):
        for i in range(lat_rows):
            window = slice(i * columns, (i + 2 * R + 1) * columns)
            mine = slice(i * columns, (i + 1) * columns)
            scores = lax.dot_general(
                queries[h][mine], keys[window, h * head : (h + 1) * head],
                (((1,), (1,)), ((), ())), preferred_element_type=jnp.float32,
            )
            weights = jnp.exp2(scores * gain).astype(jnp.bfloat16)
            sums = dot(weights, values[window, 2 * h * head : (2 * h + 2) * head])
            attended[mine, h * head : (h + 1) * head] = (
                sums[:, :head] / sums[:, head:]
            ).astype(jnp.bfloat16)

    loads[5].wait()
    mixed = embedded + dot(attended[...], out_w[...])
    loads[6].wait()
    hidden = jax.nn.gelu(dot(rms_scale(mixed).astype(jnp.bfloat16), up_w[...]))
    loads[7].wait()
    mixed = mixed + dot(hidden.astype(jnp.bfloat16), down_w[...])
    loads[8].wait()
    padded[...] = jnp.zeros_like(padded)
    padded[:, :channels] = lax.dot_general(
        rms_scale(mixed).astype(jnp.bfloat16), dec_w[...], (((1,), (1,)), ((), ())),
        preferred_element_type=jnp.float32,
    )

    turned = padded[...]
    turns = (period - token % period) % period
    for bit in range((period - 1).bit_length()):
        turned = jnp.where((turns >> bit) % 2 == 1, pltpu.roll(turned, unit << bit, 1), turned)
    split = jnp.concatenate(
        [jnp.where(in_first, turned, 0.0), jnp.where(in_first, 0.0, turned)], axis=0
    )
    coarse = split.astype(jnp.bfloat16)
    fine = (split - coarse.astype(jnp.float32)).astype(jnp.bfloat16)
    scatter = jnp.concatenate(
        [places((padded_rows, tokens), 1, 0, 0), places((padded_rows, tokens), 1, 0, 1)], axis=1
    )
    both = dot(scatter, jnp.concatenate([coarse, fine], axis=1))
    own = noise * (both[:rows, :LANES] + both[:rows, LANES:])

    piece = rows // CHUNKS
    carries = []
    for c in range(CHUNKS):
        at = slice(c * piece, (c + 1) * piece)
        carries.append(
            pltpu.make_async_remote_copy(
                src_ref=carry_out.at[at], dst_ref=carry_in.at[at], send_sem=carry_send.at[c],
                recv_sem=carry_recv.at[c], device_id=(step + 1, band), device_id_type=MESH,
            )
        )

    @pl.when(opens)
    def _():
        carry_in[...] = jnp.zeros_like(carry_in)

    partial = jnp.zeros((8, LANES), jnp.float32)
    for c, carry in enumerate(carries):
        at = slice(c * piece, (c + 1) * piece)
        pl.when(jnp.logical_not(opens))(carry.wait_recv)
        carry_out[at] = carry_in[at] + own[at]
        pl.when(jnp.logical_not(closes))(carry.start)
        renewed = anchor_rows[at] + carry_out[at]
        mismatch = renewed - states_rows[at]
        partial += jnp.sum((mismatch * mismatch).reshape(piece // 8, 8, LANES), axis=0)
        for g in range(c * piece // lat_rows, (c + 1) * piece // lat_rows):
            low = lat_rows * g - c * piece
            new_ref[0, :, LANES * g : LANES * (g + 1)] = renewed[low : low + lat_rows]

    total_rows = lat_rows * bands
    table = np.cos(np.pi * ((np.arange(total_rows) + 0.5) / total_rows - 0.5))
    lat = lax.broadcasted_iota(jnp.int32, (8, LANES), 0) % lat_rows + band * lat_rows
    area = jnp.zeros((8, LANES), jnp.float32)
    for i, value in enumerate(table):
        area = jnp.where(lat == i, float(value), area)
    partials[band] = partial * area

    parts = [
        pltpu.make_async_remote_copy(
            src_ref=partials.at[band], dst_ref=partials.at[band], send_sem=part_send.at[d - 1],
            recv_sem=part_recv.at[d - 1], device_id=(step, lax.rem(band + d, bands)),
            device_id_type=MESH,
        )
        for d in range(1, bands)
    ]
    for part in parts:
        part.start()
    for part in parts:
        part.wait_recv()
    total = jnp.sum(partials[...], axis=0)
    change_ref[0] = jnp.sum(total) * (1.0 / float(np.sum(table) * width))

    for part in parts:
        part.wait_send()
    for carry in carries:
        pl.when(jnp.logical_not(closes))(carry.wait_send)
    for_fields(lambda copy: copy.wait_send())


def local(
    sizes, states, anchor, step_index, sigmas, enc_w, noise_embed, qkv_w, out_w, up_w, down_w, dec_w
):
    _, lat_rows, width = states.shape
    channels, model = enc_w.shape
    columns = width // channels
    rows = lat_rows * width // LANES
    padded_rows = -(-rows // 16) * 16
    tokens = lat_rows * columns
    steps, bands = sizes
    f32, bf16 = jnp.float32, jnp.bfloat16
    weights = (enc_w, noise_embed, qkv_w, out_w, up_w, down_w, dec_w.T)
    hbm = pl.BlockSpec(memory_space=pl.ANY)
    smem = pl.BlockSpec(memory_space=pltpu.SMEM)
    dma = pltpu.SemaphoreType.DMA
    return pl.pallas_call(
        functools.partial(kernel, sizes),
        out_shape=(
            jax.ShapeDtypeStruct(states.shape, f32),
            jax.ShapeDtypeStruct((1,), f32),
        ),
        in_specs=[smem, smem] + [hbm] * 9,
        out_specs=(pl.BlockSpec(memory_space=pltpu.VMEM), smem),
        scratch_shapes=[
            pltpu.VMEM((lat_rows, width), f32),
            pltpu.VMEM((lat_rows, width), f32),
        ]
        + [pltpu.VMEM(w.shape, w.dtype) for w in weights]
        + [
            pltpu.VMEM((rows, LANES), f32),
            pltpu.VMEM((rows, LANES), f32),
            pltpu.VMEM((padded_rows, LANES), bf16),
            pltpu.VMEM((3, padded_rows, LANES), bf16),
            pltpu.VMEM((3 * tokens, model), bf16),
            pltpu.VMEM((3 * tokens, 2 * model), bf16),
            pltpu.VMEM((tokens, model), bf16),
            pltpu.VMEM((tokens, LANES), f32),
            pltpu.VMEM((rows, LANES), f32),
            pltpu.VMEM((rows, LANES), f32),
            pltpu.VMEM((bands, 8, LANES), f32),
            dma((9,)),
            dma((5,)),
            dma((3,)),
            dma((CHUNKS,)),
            dma((CHUNKS,)),
            dma((bands - 1,)),
            dma((bands - 1,)),
        ],
        compiler_params=pltpu.CompilerParams(
            collective_id=0, has_side_effects=True, vmem_limit_bytes=64 * 1024 * 1024
        ),
        cost_estimate=pl.CostEstimate(flops=2 * 10**9, bytes_accessed=5 * 10**6, transcendentals=10**6),
    )(step_index, sigmas, states, anchor, *weights)


def solution(mesh):
    placed = (
        P("step", "band", None), P("band", None), P("step"),
        P(), P(), P(), P(), P(), P(), P(), P(),
    )
    return jax.shard_map(
        functools.partial(local, (mesh.shape["step"], mesh.shape["band"])),
        mesh=mesh,
        in_specs=placed,
        out_specs=(P("step", "band", None), P("step")),
        check_vma=False,
    )
```

```python
import functools
import math

import jax
import jax.numpy as jnp
import numpy as np
from jax import lax
from jax.experimental import pallas as pl
from jax.experimental.pallas import tpu as pltpu
from jax.sharding import PartitionSpec as P

HEADS = 4
R = 2
LANES = 128
CHUNKS = 7

epsilon = 1e-06
score_gain = 3.0

MESH = pl.DeviceIdType.MESH


def rms_scale(values):
    return values * lax.rsqrt(jnp.mean(values * values, axis=-1, keepdims=True) + epsilon)


def dot(a, b):
    return jnp.dot(a, b, preferred_element_type=jnp.float32)


def kernel(
    sizes,
    step_index, sigmas, states_hbm, anchor_hbm, enc_hbm, embed_hbm, qkv_hbm, out_hbm, up_hbm,
    down_hbm, dec_hbm,
    new_ref, change_ref,
    states_flat, anchor_flat, enc_w, noise_embed, qkv_w, out_w, up_w, down_w, dec_w,
    states_rows, anchor_rows, sent, fields, keys, values, attended, padded,
    carry_in, carry_out, partials, load_sem, sent_sem, fields_sem, carry_send, carry_recv,
    part_send, part_recv,
):
    steps, bands = sizes
    step, band = lax.axis_index("step"), lax.axis_index("band")
    lat_rows, width = states_flat.shape
    channels, model = enc_w.shape
    columns = width // channels
    tokens = lat_rows * columns
    groups = width // LANES
    rows = states_rows.shape[0]
    padded_rows = sent.shape[0]
    head = model // HEADS
    above, below = band > 0, band < bands - 1
    opens, closes = step == 0, step == steps - 1

    pairs = (
        (states_hbm.at[0], states_flat), (anchor_hbm, anchor_flat), (enc_hbm, enc_w),
        (embed_hbm, noise_embed), (qkv_hbm, qkv_w), (out_hbm, out_w), (up_hbm, up_w),
        (down_hbm, down_w), (dec_hbm, dec_w),
    )
    loads = [pltpu.make_async_copy(a, b, load_sem.at[i]) for i, (a, b) in enumerate(pairs)]
    for load in loads:
        load.start()

    barrier = pltpu.get_barrier_semaphore()

    def greet(to_step, to_band):
        pl.semaphore_signal(barrier, inc=1, device_id=(to_step, to_band), device_id_type=MESH)

    @pl.when(step > 0)
    def _():
        greet(step - 1, band)

        @pl.when(above)
        def _():
            greet(step - 1, band - 1)

        @pl.when(below)
        def _():
            greet(step - 1, band + 1)

    for d in range(1, bands):
        greet(step, lax.rem(band + d, bands))

    def to_rows(flat, out):
        for g in range(groups):
            out[lat_rows * g : lat_rows * (g + 1), :] = flat[:, LANES * g : LANES * (g + 1)]

    loads[0].wait()
    to_rows(states_flat, states_rows)
    zero_rows = jnp.zeros((padded_rows - rows, LANES), jnp.float32)
    sent[...] = jnp.concatenate([states_rows[...], zero_rows], axis=0).astype(jnp.bfloat16)
    loads[1].wait()
    to_rows(anchor_flat, anchor_rows)

    @pl.when(opens)
    def _():
        fields[1] = jnp.concatenate([anchor_rows[...], zero_rows], axis=0).astype(jnp.bfloat16)

    onward = 1 + above.astype(jnp.int32) + below.astype(jnp.int32)
    pl.semaphore_wait(barrier, bands - 1 + jnp.where(closes, 0, onward))

    def field_copy(source, slot, sem, to_step, to_band):
        return pltpu.make_async_remote_copy(
            src_ref=source, dst_ref=fields.at[slot], send_sem=sent_sem.at[sem],
            recv_sem=fields_sem.at[slot], device_id=(to_step, to_band), device_id_type=MESH,
        )

    to_center = field_copy(sent, 1, 0, step + 1, band)
    to_above = field_copy(sent, 2, 1, step + 1, band - 1)
    to_below = field_copy(sent, 0, 2, step + 1, band + 1)
    open_above = field_copy(fields.at[1], 2, 3, step, band - 1)
    open_below = field_copy(fields.at[1], 0, 4, step, band + 1)

    def for_fields(act):
        @pl.when(jnp.logical_not(closes))
        def _():
            act(to_center)

            @pl.when(above)
            def _():
                act(to_above)

            @pl.when(below)
            def _():
                act(to_below)

        @pl.when(opens)
        def _():
            @pl.when(above)
            def _():
                act(open_above)

            @pl.when(below)
            def _():
                act(open_below)

    for_fields(lambda copy: copy.start())

    @pl.when(jnp.logical_not(above))
    def _():
        fields[0] = jnp.zeros((padded_rows, LANES), jnp.bfloat16)

    @pl.when(jnp.logical_not(below))
    def _():
        fields[2] = jnp.zeros((padded_rows, LANES), jnp.bfloat16)

    unit = math.gcd(channels, LANES)
    period = LANES // unit
    stride = pow(-(channels // unit), -1, period)

    def column_of(token):
        place, turn = token % columns, token % period
        return place - turn + (turn * stride) % period

    def places(shape, token_dim, row_dim, later):
        token = lax.broadcasted_iota(jnp.int32, shape, token_dim)
        row = lax.broadcasted_iota(jnp.int32, shape, row_dim)
        lat, column = token // columns, column_of(token)
        first = (column * channels) // LANES + later
        return (row == first * lat_rows + lat).astype(jnp.float32).astype(jnp.bfloat16)

    gather_first = places((tokens, padded_rows), 0, 1, 0)
    gather_next = places((tokens, padded_rows), 0, 1, 1)
    token = lax.broadcasted_iota(jnp.int32, (tokens, LANES), 0)
    lane = lax.broadcasted_iota(jnp.int32, (tokens, LANES), 1)
    in_first = lane >= (column_of(token) * channels) % LANES

    noise = sigmas[step_index[0]]
    loads[2].wait()
    loads[3].wait()
    offset = jnp.log(jnp.full((1, model), noise, jnp.float32)) * noise_embed[...].reshape(1, model)
    loads[4].wait()

    def embed(slot):
        packed = fields[slot]
        picked = jnp.where(in_first, dot(gather_first, packed), dot(gather_next, packed))
        turned = pltpu.roll(picked, 0, 1, stride=unit, stride_axis=0)
        return dot(turned[:, :channels].astype(jnp.bfloat16), enc_w[...]) + offset

    def keep_key_value(slot, key_value, valid):
        at = slice(slot * tokens, (slot + 1) * tokens)
        for h in range(HEADS):
            here = slice(h * head, (h + 1) * head)
            keys[at, here] = rms_scale(key_value[:, here]).astype(jnp.bfloat16)
            value = key_value[:, model + h * head : model + (h + 1) * head]
            ones = jnp.ones((tokens, head), jnp.float32)
            if valid is not None:
                value, ones = value * valid, ones * valid
            values[at, 2 * h * head : (2 * h + 1) * head] = value.astype(jnp.bfloat16)
            values[at, (2 * h + 1) * head : (2 * h + 2) * head] = ones.astype(jnp.bfloat16)

    @pl.when(jnp.logical_not(opens))
    def _():
        to_center.wait_recv()

    embedded = embed(1)
    projected = dot(rms_scale(embedded).astype(jnp.bfloat16), qkv_w[...])
    queries = [
        rms_scale(projected[:, h * head : (h + 1) * head]).astype(jnp.bfloat16)
        for h in range(HEADS)
    ]
    keep_key_value(1, projected[:, model:], None)

    for slot, there, copy in ((0, above, to_below), (2, below, to_above)):
        pl.when(there)(copy.wait_recv)
        normed = rms_scale(embed(slot)).astype(jnp.bfloat16)
        keep_key_value(slot, dot(normed, qkv_w[:, model:]), there.astype(jnp.float32))

    gain = score_gain / math.sqrt(head) * math.log2(math.e)
    for h in range(HEADS):
        for i in range(lat_rows):
            window = slice(i * columns, (i + 2 * R + 1) * columns)
            mine = slice(i * columns, (i + 1) * columns)
            scores = lax.dot_general(
                queries[h][mine], keys[window, h * head : (h + 1) * head],
                (((1,), (1,)), ((), ())), preferred_element_type=jnp.float32,
            )
            weights = jnp.exp2(scores * gain).astype(jnp.bfloat16)
            sums = dot(weights, values[window, 2 * h * head : (2 * h + 2) * head])
            attended[mine, h * head : (h + 1) * head] = (
                sums[:, :head] / sums[:, head:]
            ).astype(jnp.bfloat16)

    loads[5].wait()
    mixed = embedded + dot(attended[...], out_w[...])
    loads[6].wait()
    hidden = jax.nn.gelu(dot(rms_scale(mixed).astype(jnp.bfloat16), up_w[...]))
    loads[7].wait()
    mixed = mixed + dot(hidden.astype(jnp.bfloat16), down_w[...])
    loads[8].wait()
    padded[...] = jnp.zeros_like(padded)
    padded[:, :channels] = lax.dot_general(
        rms_scale(mixed).astype(jnp.bfloat16), dec_w[...], (((1,), (1,)), ((), ())),
        preferred_element_type=jnp.float32,
    )

    turned = padded[...]
    turns = (period - token % period) % period
    for bit in range((period - 1).bit_length()):
        turned = jnp.where((turns >> bit) % 2 == 1, pltpu.roll(turned, unit << bit, 1), turned)
    split = jnp.concatenate(
        [jnp.where(in_first, turned, 0.0), jnp.where(in_first, 0.0, turned)], axis=0
    )
    coarse = split.astype(jnp.bfloat16)
    fine = (split - coarse.astype(jnp.float32)).astype(jnp.bfloat16)
    scatter = jnp.concatenate(
        [places((padded_rows, tokens), 1, 0, 0), places((padded_rows, tokens), 1, 0, 1)], axis=1
    )
    both = dot(scatter, jnp.concatenate([coarse, fine], axis=1))
    own = noise * (both[:rows, :LANES] + both[:rows, LANES:])

    piece = rows // CHUNKS
    carries = []
    for c in range(CHUNKS):
        at = slice(c * piece, (c + 1) * piece)
        carries.append(
            pltpu.make_async_remote_copy(
                src_ref=carry_out.at[at], dst_ref=carry_in.at[at], send_sem=carry_send.at[c],
                recv_sem=carry_recv.at[c], device_id=(step + 1, band), device_id_type=MESH,
            )
        )

    @pl.when(opens)
    def _():
        carry_in[...] = jnp.zeros_like(carry_in)

    partial = jnp.zeros((8, LANES), jnp.float32)
    for c, carry in enumerate(carries):
        at = slice(c * piece, (c + 1) * piece)
        pl.when(jnp.logical_not(opens))(carry.wait_recv)
        carry_out[at] = carry_in[at] + own[at]
        pl.when(jnp.logical_not(closes))(carry.start)
        renewed = anchor_rows[at] + carry_out[at]
        mismatch = renewed - states_rows[at]
        partial += jnp.sum((mismatch * mismatch).reshape(piece // 8, 8, LANES), axis=0)
        for g in range(c * piece // lat_rows, (c + 1) * piece // lat_rows):
            low = lat_rows * g - c * piece
            new_ref[0, :, LANES * g : LANES * (g + 1)] = renewed[low : low + lat_rows]

    total_rows = lat_rows * bands
    table = np.cos(np.pi * ((np.arange(total_rows) + 0.5) / total_rows - 0.5))
    lat = lax.broadcasted_iota(jnp.int32, (8, LANES), 0) % lat_rows + band * lat_rows
    area = jnp.zeros((8, LANES), jnp.float32)
    for i, value in enumerate(table):
        area = jnp.where(lat == i, float(value), area)
    partials[band] = partial * area

    parts = [
        pltpu.make_async_remote_copy(
            src_ref=partials.at[band], dst_ref=partials.at[band], send_sem=part_send.at[d - 1],
            recv_sem=part_recv.at[d - 1], device_id=(step, lax.rem(band + d, bands)),
            device_id_type=MESH,
        )
        for d in range(1, bands)
    ]
    for part in parts:
        part.start()
    for part in parts:
        part.wait_recv()
    total = jnp.sum(partials[...], axis=0)
    change_ref[0] = jnp.sum(total) * (1.0 / float(np.sum(table) * width))

    for part in parts:
        part.wait_send()
    for carry in carries:
        pl.when(jnp.logical_not(closes))(carry.wait_send)
    for_fields(lambda copy: copy.wait_send())


def local(
    sizes, states, anchor, step_index, sigmas, enc_w, noise_embed, qkv_w, out_w, up_w, down_w, dec_w
):
    _, lat_rows, width = states.shape
    channels, model = enc_w.shape
    columns = width // channels
    rows = lat_rows * width // LANES
    padded_rows = -(-rows // 16) * 16
    tokens = lat_rows * columns
    steps, bands = sizes
    f32, bf16 = jnp.float32, jnp.bfloat16
    weights = (enc_w, noise_embed, qkv_w, out_w, up_w, down_w, dec_w.T)
    hbm = pl.BlockSpec(memory_space=pl.ANY)
    smem = pl.BlockSpec(memory_space=pltpu.SMEM)
    dma = pltpu.SemaphoreType.DMA
    return pl.pallas_call(
        functools.partial(kernel, sizes),
        out_shape=(
            pltpu.VMEM(states.shape, f32),
            jax.ShapeDtypeStruct((1,), f32),
        ),
        in_specs=[smem, smem] + [hbm] * 9,
        out_specs=(pl.BlockSpec(memory_space=pltpu.VMEM), smem),
        scratch_shapes=[
            pltpu.VMEM((lat_rows, width), f32),
            pltpu.VMEM((lat_rows, width), f32),
        ]
        + [pltpu.VMEM(w.shape, w.dtype) for w in weights]
        + [
            pltpu.VMEM((rows, LANES), f32),
            pltpu.VMEM((rows, LANES), f32),
            pltpu.VMEM((padded_rows, LANES), bf16),
            pltpu.VMEM((3, padded_rows, LANES), bf16),
            pltpu.VMEM((3 * tokens, model), bf16),
            pltpu.VMEM((3 * tokens, 2 * model), bf16),
            pltpu.VMEM((tokens, model), bf16),
            pltpu.VMEM((tokens, LANES), f32),
            pltpu.VMEM((rows, LANES), f32),
            pltpu.VMEM((rows, LANES), f32),
            pltpu.VMEM((bands, 8, LANES), f32),
            dma((9,)),
            dma((5,)),
            dma((3,)),
            dma((CHUNKS,)),
            dma((CHUNKS,)),
            dma((bands - 1,)),
            dma((bands - 1,)),
        ],
        compiler_params=pltpu.CompilerParams(
            collective_id=0, has_side_effects=True, vmem_limit_bytes=(65536 - 512) * 1024
        ),
        cost_estimate=pl.CostEstimate(flops=2 * 10**9, bytes_accessed=5 * 10**6, transcendentals=10**6),
    )(step_index, sigmas, states, anchor, *weights)


def solution(mesh):
    placed = (
        P("step", "band", None), P("band", None), P("step"),
        P(), P(), P(), P(), P(), P(), P(), P(),
    )
    return jax.shard_map(
        functools.partial(local, (mesh.shape["step"], mesh.shape["band"])),
        mesh=mesh,
        in_specs=placed,
        out_specs=(P("step", "band", None), P("step")),
        check_vma=False,
    )
```

```python
import functools
import math

import jax
import jax.numpy as jnp
import numpy as np
from jax import lax
from jax.experimental import pallas as pl
from jax.experimental.pallas import tpu as pltpu
from jax.sharding import PartitionSpec as P

HEADS = 4
R = 2
LANES = 128
CHUNKS = 7

epsilon = 1e-06
score_gain = 3.0

MESH = pl.DeviceIdType.MESH


def rms_scale(values):
    return values * lax.rsqrt(jnp.mean(values * values, axis=-1, keepdims=True) + epsilon)


def dot(a, b):
    return jnp.dot(a, b, preferred_element_type=jnp.float32)


def kernel(
    sizes,
    step_index, sigmas, states_hbm, anchor_hbm, enc_hbm, embed_hbm, qkv_hbm, out_hbm, up_hbm,
    down_hbm, dec_hbm,
    new_ref, change_ref,
    states_flat, anchor_flat, enc_w, noise_embed, qkv_w, out_w, up_w, down_w, dec_w,
    states_rows, anchor_rows, sent, fields, keys, values, attended, padded,
    carry_in, carry_out, partials, load_sem, sent_sem, fields_sem, carry_send, carry_recv,
    part_send, part_recv,
):
    steps, bands = sizes
    step, band = lax.axis_index("step"), lax.axis_index("band")
    lat_rows, width = states_flat.shape
    channels, model = enc_w.shape
    columns = width // channels
    tokens = lat_rows * columns
    groups = width // LANES
    rows = states_rows.shape[0]
    padded_rows = sent.shape[0]
    head = model // HEADS
    above, below = band > 0, band < bands - 1
    opens, closes = step == 0, step == steps - 1

    pairs = (
        (states_hbm.at[0], states_flat), (anchor_hbm, anchor_flat), (enc_hbm, enc_w),
        (embed_hbm, noise_embed), (qkv_hbm, qkv_w), (out_hbm, out_w), (up_hbm, up_w),
        (down_hbm, down_w), (dec_hbm, dec_w),
    )
    loads = [pltpu.make_async_copy(a, b, load_sem.at[i]) for i, (a, b) in enumerate(pairs)]
    for load in loads:
        load.start()

    barrier = pltpu.get_barrier_semaphore()

    def greet(to_step, to_band):
        pl.semaphore_signal(barrier, inc=1, device_id=(to_step, to_band), device_id_type=MESH)

    @pl.when(step > 0)
    def _():
        greet(step - 1, band)

        @pl.when(above)
        def _():
            greet(step - 1, band - 1)

        @pl.when(below)
        def _():
            greet(step - 1, band + 1)

    for d in range(1, bands):
        greet(step, lax.rem(band + d, bands))

    def to_rows(flat, out):
        for g in range(groups):
            out[lat_rows * g : lat_rows * (g + 1), :] = flat[:, LANES * g : LANES * (g + 1)]

    loads[0].wait()
    to_rows(states_flat, states_rows)
    zero_rows = jnp.zeros((padded_rows - rows, LANES), jnp.float32)
    sent[...] = jnp.concatenate([states_rows[...], zero_rows], axis=0).astype(jnp.bfloat16)
    loads[1].wait()
    to_rows(anchor_flat, anchor_rows)

    @pl.when(opens)
    def _():
        fields[1] = jnp.concatenate([anchor_rows[...], zero_rows], axis=0).astype(jnp.bfloat16)

    onward = 1 + above.astype(jnp.int32) + below.astype(jnp.int32)
    pl.semaphore_wait(barrier, bands - 1 + jnp.where(closes, 0, onward))

    def field_copy(source, slot, sem, to_step, to_band):
        return pltpu.make_async_remote_copy(
            src_ref=source, dst_ref=fields.at[slot], send_sem=sent_sem.at[sem],
            recv_sem=fields_sem.at[slot], device_id=(to_step, to_band), device_id_type=MESH,
        )

    to_center = field_copy(sent, 1, 0, step + 1, band)
    to_above = field_copy(sent, 2, 1, step + 1, band - 1)
    to_below = field_copy(sent, 0, 2, step + 1, band + 1)
    open_above = field_copy(fields.at[1], 2, 3, step, band - 1)
    open_below = field_copy(fields.at[1], 0, 4, step, band + 1)

    def for_fields(act):
        @pl.when(jnp.logical_not(closes))
        def _():
            act(to_center)

            @pl.when(above)
            def _():
                act(to_above)

            @pl.when(below)
            def _():
                act(to_below)

        @pl.when(opens)
        def _():
            @pl.when(above)
            def _():
                act(open_above)

            @pl.when(below)
            def _():
                act(open_below)

    for_fields(lambda copy: copy.start())

    @pl.when(jnp.logical_not(above))
    def _():
        fields[0] = jnp.zeros((padded_rows, LANES), jnp.bfloat16)

    @pl.when(jnp.logical_not(below))
    def _():
        fields[2] = jnp.zeros((padded_rows, LANES), jnp.bfloat16)

    unit = math.gcd(channels, LANES)
    period = LANES // unit
    stride = pow(-(channels // unit), -1, period)

    def column_of(token):
        place, turn = token % columns, token % period
        return place - turn + (turn * stride) % period

    def places(shape, token_dim, row_dim, later):
        token = lax.broadcasted_iota(jnp.int32, shape, token_dim)
        row = lax.broadcasted_iota(jnp.int32, shape, row_dim)
        lat, column = token // columns, column_of(token)
        first = (column * channels) // LANES + later
        return (row == first * lat_rows + lat).astype(jnp.float32).astype(jnp.bfloat16)

    gather_first = places((tokens, padded_rows), 0, 1, 0)
    gather_next = places((tokens, padded_rows), 0, 1, 1)
    token = lax.broadcasted_iota(jnp.int32, (tokens, LANES), 0)
    lane = lax.broadcasted_iota(jnp.int32, (tokens, LANES), 1)
    in_first = lane >= (column_of(token) * channels) % LANES

    noise = sigmas[step_index[0]]
    loads[2].wait()
    loads[3].wait()
    offset = jnp.log(jnp.full((1, model), noise, jnp.float32)) * noise_embed[...].reshape(1, model)
    loads[4].wait()

    def embed(slot):
        packed = fields[slot]
        picked = jnp.where(in_first, dot(gather_first, packed), dot(gather_next, packed))
        turned = pltpu.roll(picked, 0, 1, stride=unit, stride_axis=0)
        return dot(turned[:, :channels].astype(jnp.bfloat16), enc_w[...]) + offset

    def keep_key_value(slot, key_value, valid):
        at = slice(slot * tokens, (slot + 1) * tokens)
        for h in range(HEADS):
            here = slice(h * head, (h + 1) * head)
            keys[at, here] = rms_scale(key_value[:, here]).astype(jnp.bfloat16)
            value = key_value[:, model + h * head : model + (h + 1) * head]
            ones = jnp.ones((tokens, head), jnp.float32)
            if valid is not None:
                value, ones = value * valid, ones * valid
            values[at, 2 * h * head : (2 * h + 1) * head] = value.astype(jnp.bfloat16)
            values[at, (2 * h + 1) * head : (2 * h + 2) * head] = ones.astype(jnp.bfloat16)

    @pl.when(jnp.logical_not(opens))
    def _():
        to_center.wait_recv()

    embedded = embed(1)
    projected = dot(rms_scale(embedded).astype(jnp.bfloat16), qkv_w[...])
    queries = [
        rms_scale(projected[:, h * head : (h + 1) * head]).astype(jnp.bfloat16)
        for h in range(HEADS)
    ]
    keep_key_value(1, projected[:, model:], None)

    sides = ((0, above, to_below), (2, below, to_above))
    normed = []
    for slot, there, copy in sides:
        pl.when(there)(copy.wait_recv)
        normed.append(rms_scale(embed(slot)).astype(jnp.bfloat16))
    key_value = dot(jnp.concatenate(normed, axis=0), qkv_w[:, model:])
    for n, (slot, there, _) in enumerate(sides):
        keep_key_value(slot, key_value[n * tokens : (n + 1) * tokens], there.astype(jnp.float32))

    gain = score_gain / math.sqrt(head) * math.log2(math.e)
    def weigh(query, h, low, high):
        window = slice(low * columns, high * columns)
        scores = lax.dot_general(
            query, keys[window, h * head : (h + 1) * head],
            (((1,), (1,)), ((), ())), preferred_element_type=jnp.float32,
        )
        weights = jnp.exp2(scores * gain).astype(jnp.bfloat16)
        return dot(weights, values[window, 2 * h * head : (2 * h + 2) * head])

    for h in range(HEADS):
        shared = weigh(queries[h], h, lat_rows - 1, 2 * R + 1)
        for i in range(lat_rows):
            mine = slice(i * columns, (i + 1) * columns)
            sums = shared[mine]
            for low, high in ((i, lat_rows - 1), (2 * R + 1, i + 2 * R + 1)):
                if low < high:
                    sums = sums + weigh(queries[h][mine], h, low, high)
            attended[mine, h * head : (h + 1) * head] = (
                sums[:, :head] / sums[:, head:]
            ).astype(jnp.bfloat16)

    loads[5].wait()
    mixed = embedded + dot(attended[...], out_w[...])
    loads[6].wait()
    hidden = jax.nn.gelu(dot(rms_scale(mixed).astype(jnp.bfloat16), up_w[...]))
    loads[7].wait()
    mixed = mixed + dot(hidden.astype(jnp.bfloat16), down_w[...])
    loads[8].wait()
    padded[...] = jnp.zeros_like(padded)
    padded[:, :channels] = lax.dot_general(
        rms_scale(mixed).astype(jnp.bfloat16), dec_w[...], (((1,), (1,)), ((), ())),
        preferred_element_type=jnp.float32,
    )

    turned = padded[...]
    turns = (period - token % period) % period
    for bit in range((period - 1).bit_length()):
        turned = jnp.where((turns >> bit) % 2 == 1, pltpu.roll(turned, unit << bit, 1), turned)
    split = jnp.concatenate(
        [jnp.where(in_first, turned, 0.0), jnp.where(in_first, 0.0, turned)], axis=0
    )
    coarse = split.astype(jnp.bfloat16)
    fine = (split - coarse.astype(jnp.float32)).astype(jnp.bfloat16)
    scatter = jnp.concatenate(
        [places((padded_rows, tokens), 1, 0, 0), places((padded_rows, tokens), 1, 0, 1)], axis=1
    )
    both = dot(scatter, jnp.concatenate([coarse, fine], axis=1))
    own = noise * (both[:rows, :LANES] + both[:rows, LANES:])

    piece = rows // CHUNKS
    carries = []
    for c in range(CHUNKS):
        at = slice(c * piece, (c + 1) * piece)
        carries.append(
            pltpu.make_async_remote_copy(
                src_ref=carry_out.at[at], dst_ref=carry_in.at[at], send_sem=carry_send.at[c],
                recv_sem=carry_recv.at[c], device_id=(step + 1, band), device_id_type=MESH,
            )
        )

    @pl.when(opens)
    def _():
        carry_in[...] = jnp.zeros_like(carry_in)

    partial = jnp.zeros((8, LANES), jnp.float32)
    for c, carry in enumerate(carries):
        at = slice(c * piece, (c + 1) * piece)
        pl.when(jnp.logical_not(opens))(carry.wait_recv)
        carry_out[at] = carry_in[at] + own[at]
        pl.when(jnp.logical_not(closes))(carry.start)
        renewed = anchor_rows[at] + carry_out[at]
        mismatch = renewed - states_rows[at]
        partial += jnp.sum((mismatch * mismatch).reshape(piece // 8, 8, LANES), axis=0)
        for g in range(c * piece // lat_rows, (c + 1) * piece // lat_rows):
            low = lat_rows * g - c * piece
            new_ref[0, :, LANES * g : LANES * (g + 1)] = renewed[low : low + lat_rows]

    total_rows = lat_rows * bands
    table = np.cos(np.pi * ((np.arange(total_rows) + 0.5) / total_rows - 0.5))
    lat = lax.broadcasted_iota(jnp.int32, (8, LANES), 0) % lat_rows + band * lat_rows
    area = jnp.zeros((8, LANES), jnp.float32)
    for i, value in enumerate(table):
        area = jnp.where(lat == i, float(value), area)
    partials[band] = partial * area

    parts = [
        pltpu.make_async_remote_copy(
            src_ref=partials.at[band], dst_ref=partials.at[band], send_sem=part_send.at[d - 1],
            recv_sem=part_recv.at[d - 1], device_id=(step, lax.rem(band + d, bands)),
            device_id_type=MESH,
        )
        for d in range(1, bands)
    ]
    for part in parts:
        part.start()
    for part in parts:
        part.wait_recv()
    total = jnp.sum(partials[...], axis=0)
    change_ref[0] = jnp.sum(total) * (1.0 / float(np.sum(table) * width))

    for part in parts:
        part.wait_send()
    for carry in carries:
        pl.when(jnp.logical_not(closes))(carry.wait_send)
    for_fields(lambda copy: copy.wait_send())


def local(
    sizes, states, anchor, step_index, sigmas, enc_w, noise_embed, qkv_w, out_w, up_w, down_w, dec_w
):
    _, lat_rows, width = states.shape
    channels, model = enc_w.shape
    columns = width // channels
    rows = lat_rows * width // LANES
    padded_rows = -(-rows // 16) * 16
    tokens = lat_rows * columns
    steps, bands = sizes
    f32, bf16 = jnp.float32, jnp.bfloat16
    weights = (enc_w, noise_embed, qkv_w, out_w, up_w, down_w, dec_w.T)
    hbm = pl.BlockSpec(memory_space=pl.ANY)
    smem = pl.BlockSpec(memory_space=pltpu.SMEM)
    dma = pltpu.SemaphoreType.DMA
    return pl.pallas_call(
        functools.partial(kernel, sizes),
        out_shape=(
            pltpu.VMEM(states.shape, f32),
            jax.ShapeDtypeStruct((1,), f32),
        ),
        in_specs=[smem, smem] + [hbm] * 9,
        out_specs=(pl.BlockSpec(memory_space=pltpu.VMEM), smem),
        scratch_shapes=[
            pltpu.VMEM((lat_rows, width), f32),
            pltpu.VMEM((lat_rows, width), f32),
        ]
        + [pltpu.VMEM(w.shape, w.dtype) for w in weights]
        + [
            pltpu.VMEM((rows, LANES), f32),
            pltpu.VMEM((rows, LANES), f32),
            pltpu.VMEM((padded_rows, LANES), bf16),
            pltpu.VMEM((3, padded_rows, LANES), bf16),
            pltpu.VMEM((3 * tokens, model), bf16),
            pltpu.VMEM((3 * tokens, 2 * model), bf16),
            pltpu.VMEM((tokens, model), bf16),
            pltpu.VMEM((tokens, LANES), f32),
            pltpu.VMEM((rows, LANES), f32),
            pltpu.VMEM((rows, LANES), f32),
            pltpu.VMEM((bands, 8, LANES), f32),
            dma((9,)),
            dma((5,)),
            dma((3,)),
            dma((CHUNKS,)),
            dma((CHUNKS,)),
            dma((bands - 1,)),
            dma((bands - 1,)),
        ],
        compiler_params=pltpu.CompilerParams(
            collective_id=0, has_side_effects=True, vmem_limit_bytes=(65536 - 512) * 1024
        ),
        cost_estimate=pl.CostEstimate(flops=2 * 10**9, bytes_accessed=5 * 10**6, transcendentals=10**6),
    )(step_index, sigmas, states, anchor, *weights)


def solution(mesh):
    placed = (
        P("step", "band", None), P("band", None), P("step"),
        P(), P(), P(), P(), P(), P(), P(), P(),
    )
    return jax.shard_map(
        functools.partial(local, (mesh.shape["step"], mesh.shape["band"])),
        mesh=mesh,
        in_specs=placed,
        out_specs=(P("step", "band", None), P("step")),
        check_vma=False,
    )
```

```python
import functools
import math

import jax
import jax.numpy as jnp
import numpy as np
from jax import lax
from jax.experimental import pallas as pl
from jax.experimental.pallas import tpu as pltpu
from jax.sharding import PartitionSpec as P

HEADS = 4
R = 2
LANES = 128
CHUNKS = 21

epsilon = 1e-06
score_gain = 3.0

MESH = pl.DeviceIdType.MESH


def rms_scale(values):
    return values * lax.rsqrt(jnp.mean(values * values, axis=-1, keepdims=True) + epsilon)


def dot(a, b):
    return jnp.dot(a, b, preferred_element_type=jnp.float32)


def kernel(
    sizes,
    step_index, sigmas, states_hbm, anchor_hbm, enc_hbm, embed_hbm, qkv_hbm, out_hbm, up_hbm,
    down_hbm, dec_hbm,
    new_ref, change_ref,
    states_flat, anchor_flat, enc_w, noise_embed, qkv_w, out_w, up_w, down_w, dec_w,
    states_rows, anchor_rows, sent, fields, keys, values, attended, padded,
    carry_in, carry_out, partials, load_sem, sent_sem, fields_sem, carry_send, carry_recv,
    part_send, part_recv,
):
    steps, bands = sizes
    step, band = lax.axis_index("step"), lax.axis_index("band")
    lat_rows, width = states_flat.shape
    channels, model = enc_w.shape
    columns = width // channels
    tokens = lat_rows * columns
    groups = width // LANES
    rows = states_rows.shape[0]
    padded_rows = sent.shape[0]
    head = model // HEADS
    above, below = band > 0, band < bands - 1
    opens, closes = step == 0, step == steps - 1

    pairs = (
        (states_hbm.at[0], states_flat), (anchor_hbm, anchor_flat), (enc_hbm, enc_w),
        (embed_hbm, noise_embed), (qkv_hbm, qkv_w), (out_hbm, out_w), (up_hbm, up_w),
        (down_hbm, down_w), (dec_hbm, dec_w),
    )
    loads = [pltpu.make_async_copy(a, b, load_sem.at[i]) for i, (a, b) in enumerate(pairs)]
    for load in loads:
        load.start()

    barrier = pltpu.get_barrier_semaphore()

    def greet(to_step, to_band):
        pl.semaphore_signal(barrier, inc=1, device_id=(to_step, to_band), device_id_type=MESH)

    @pl.when(step > 0)
    def _():
        greet(step - 1, band)

        @pl.when(above)
        def _():
            greet(step - 1, band - 1)

        @pl.when(below)
        def _():
            greet(step - 1, band + 1)

    for d in range(1, bands):
        greet(step, lax.rem(band + d, bands))

    def to_rows(flat, out):
        for g in range(groups):
            out[lat_rows * g : lat_rows * (g + 1), :] = flat[:, LANES * g : LANES * (g + 1)]

    loads[0].wait()
    to_rows(states_flat, states_rows)
    zero_rows = jnp.zeros((padded_rows - rows, LANES), jnp.float32)
    sent[...] = jnp.concatenate([states_rows[...], zero_rows], axis=0).astype(jnp.bfloat16)
    loads[1].wait()
    to_rows(anchor_flat, anchor_rows)

    @pl.when(opens)
    def _():
        fields[1] = jnp.concatenate([anchor_rows[...], zero_rows], axis=0).astype(jnp.bfloat16)

    onward = 1 + above.astype(jnp.int32) + below.astype(jnp.int32)
    pl.semaphore_wait(barrier, bands - 1 + jnp.where(closes, 0, onward))

    def field_copy(source, slot, sem, to_step, to_band):
        return pltpu.make_async_remote_copy(
            src_ref=source, dst_ref=fields.at[slot], send_sem=sent_sem.at[sem],
            recv_sem=fields_sem.at[slot], device_id=(to_step, to_band), device_id_type=MESH,
        )

    to_center = field_copy(sent, 1, 0, step + 1, band)
    to_above = field_copy(sent, 2, 1, step + 1, band - 1)
    to_below = field_copy(sent, 0, 2, step + 1, band + 1)
    open_above = field_copy(fields.at[1], 2, 3, step, band - 1)
    open_below = field_copy(fields.at[1], 0, 4, step, band + 1)

    def for_fields(act):
        @pl.when(jnp.logical_not(closes))
        def _():
            act(to_center)

            @pl.when(above)
            def _():
                act(to_above)

            @pl.when(below)
            def _():
                act(to_below)

        @pl.when(opens)
        def _():
            @pl.when(above)
            def _():
                act(open_above)

            @pl.when(below)
            def _():
                act(open_below)

    for_fields(lambda copy: copy.start())

    @pl.when(jnp.logical_not(above))
    def _():
        fields[0] = jnp.zeros((padded_rows, LANES), jnp.bfloat16)

    @pl.when(jnp.logical_not(below))
    def _():
        fields[2] = jnp.zeros((padded_rows, LANES), jnp.bfloat16)

    unit = math.gcd(channels, LANES)
    period = LANES // unit
    stride = pow(-(channels // unit), -1, period)

    def column_of(token):
        place, turn = token % columns, token % period
        return place - turn + (turn * stride) % period

    def places(shape, token_dim, row_dim, later):
        token = lax.broadcasted_iota(jnp.int32, shape, token_dim)
        row = lax.broadcasted_iota(jnp.int32, shape, row_dim)
        lat, column = token // columns, column_of(token)
        first = (column * channels) // LANES + later
        return (row == first * lat_rows + lat).astype(jnp.float32).astype(jnp.bfloat16)

    gather_first = places((tokens, padded_rows), 0, 1, 0)
    gather_next = places((tokens, padded_rows), 0, 1, 1)
    token = lax.broadcasted_iota(jnp.int32, (tokens, LANES), 0)
    lane = lax.broadcasted_iota(jnp.int32, (tokens, LANES), 1)
    in_first = lane >= (column_of(token) * channels) % LANES

    noise = sigmas[step_index[0]]
    loads[2].wait()
    loads[3].wait()
    offset = jnp.log(jnp.full((1, model), noise, jnp.float32)) * noise_embed[...].reshape(1, model)
    loads[4].wait()

    def embed(slot):
        packed = fields[slot]
        picked = jnp.where(in_first, dot(gather_first, packed), dot(gather_next, packed))
        turned = pltpu.roll(picked, 0, 1, stride=unit, stride_axis=0)
        return dot(turned[:, :channels].astype(jnp.bfloat16), enc_w[...]) + offset

    def keep_key_value(slot, key_value, valid):
        at = slice(slot * tokens, (slot + 1) * tokens)
        for h in range(HEADS):
            here = slice(h * head, (h + 1) * head)
            keys[at, here] = rms_scale(key_value[:, here]).astype(jnp.bfloat16)
            value = key_value[:, model + h * head : model + (h + 1) * head]
            ones = jnp.ones((tokens, head), jnp.float32)
            if valid is not None:
                value, ones = value * valid, ones * valid
            values[at, 2 * h * head : (2 * h + 1) * head] = value.astype(jnp.bfloat16)
            values[at, (2 * h + 1) * head : (2 * h + 2) * head] = ones.astype(jnp.bfloat16)

    @pl.when(jnp.logical_not(opens))
    def _():
        to_center.wait_recv()

    embedded = embed(1)
    projected = dot(rms_scale(embedded).astype(jnp.bfloat16), qkv_w[...])
    queries = [
        rms_scale(projected[:, h * head : (h + 1) * head]).astype(jnp.bfloat16)
        for h in range(HEADS)
    ]
    keep_key_value(1, projected[:, model:], None)

    for slot, there, copy in ((0, above, to_below), (2, below, to_above)):
        pl.when(there)(copy.wait_recv)
        normed = rms_scale(embed(slot)).astype(jnp.bfloat16)
        keep_key_value(slot, dot(normed, qkv_w[:, model:]), there.astype(jnp.float32))

    gain = score_gain / math.sqrt(head) * math.log2(math.e)
    for h in range(HEADS):
        for i in range(lat_rows):
            window = slice(i * columns, (i + 2 * R + 1) * columns)
            mine = slice(i * columns, (i + 1) * columns)
            scores = lax.dot_general(
                queries[h][mine], keys[window, h * head : (h + 1) * head],
                (((1,), (1,)), ((), ())), preferred_element_type=jnp.float32,
            )
            weights = jnp.exp2(scores * gain).astype(jnp.bfloat16)
            sums = dot(weights, values[window, 2 * h * head : (2 * h + 2) * head])
            attended[mine, h * head : (h + 1) * head] = (
                sums[:, :head] / sums[:, head:]
            ).astype(jnp.bfloat16)

    loads[5].wait()
    mixed = embedded + dot(attended[...], out_w[...])
    loads[6].wait()
    hidden = jax.nn.gelu(dot(rms_scale(mixed).astype(jnp.bfloat16), up_w[...]))
    loads[7].wait()
    mixed = mixed + dot(hidden.astype(jnp.bfloat16), down_w[...])
    loads[8].wait()
    padded[...] = jnp.zeros_like(padded)
    padded[:, :channels] = lax.dot_general(
        rms_scale(mixed).astype(jnp.bfloat16), dec_w[...], (((1,), (1,)), ((), ())),
        preferred_element_type=jnp.float32,
    )

    turned = padded[...]
    turns = (period - token % period) % period
    for bit in range((period - 1).bit_length()):
        turned = jnp.where((turns >> bit) % 2 == 1, pltpu.roll(turned, unit << bit, 1), turned)
    split = jnp.concatenate(
        [jnp.where(in_first, turned, 0.0), jnp.where(in_first, 0.0, turned)], axis=0
    )
    coarse = split.astype(jnp.bfloat16)
    fine = (split - coarse.astype(jnp.float32)).astype(jnp.bfloat16)
    scatter = jnp.concatenate(
        [places((padded_rows, tokens), 1, 0, 0), places((padded_rows, tokens), 1, 0, 1)], axis=1
    )
    both = dot(scatter, jnp.concatenate([coarse, fine], axis=1))
    own = noise * (both[:rows, :LANES] + both[:rows, LANES:])

    piece = rows // CHUNKS
    carries = []
    for c in range(CHUNKS):
        at = slice(c * piece, (c + 1) * piece)
        carries.append(
            pltpu.make_async_remote_copy(
                src_ref=carry_out.at[at], dst_ref=carry_in.at[at], send_sem=carry_send.at[c],
                recv_sem=carry_recv.at[c], device_id=(step + 1, band), device_id_type=MESH,
            )
        )

    @pl.when(opens)
    def _():
        carry_in[...] = jnp.zeros_like(carry_in)

    partial = jnp.zeros((8, LANES), jnp.float32)
    for c, carry in enumerate(carries):
        at = slice(c * piece, (c + 1) * piece)
        pl.when(jnp.logical_not(opens))(carry.wait_recv)
        carry_out[at] = carry_in[at] + own[at]
        pl.when(jnp.logical_not(closes))(carry.start)
        renewed = anchor_rows[at] + carry_out[at]
        mismatch = renewed - states_rows[at]
        partial += jnp.sum((mismatch * mismatch).reshape(piece // 8, 8, LANES), axis=0)
        for g in range(c * piece // lat_rows, (c + 1) * piece // lat_rows):
            low = lat_rows * g - c * piece
            new_ref[0, :, LANES * g : LANES * (g + 1)] = renewed[low : low + lat_rows]

    total_rows = lat_rows * bands
    table = np.cos(np.pi * ((np.arange(total_rows) + 0.5) / total_rows - 0.5))
    lat = lax.broadcasted_iota(jnp.int32, (8, LANES), 0) % lat_rows + band * lat_rows
    area = jnp.zeros((8, LANES), jnp.float32)
    for i, value in enumerate(table):
        area = jnp.where(lat == i, float(value), area)
    partials[band] = partial * area

    parts = [
        pltpu.make_async_remote_copy(
            src_ref=partials.at[band], dst_ref=partials.at[band], send_sem=part_send.at[d - 1],
            recv_sem=part_recv.at[d - 1], device_id=(step, lax.rem(band + d, bands)),
            device_id_type=MESH,
        )
        for d in range(1, bands)
    ]
    for part in parts:
        part.start()
    for part in parts:
        part.wait_recv()
    total = jnp.sum(partials[...], axis=0)
    change_ref[0] = jnp.sum(total) * (1.0 / float(np.sum(table) * width))

    for part in parts:
        part.wait_send()
    for carry in carries:
        pl.when(jnp.logical_not(closes))(carry.wait_send)
    for_fields(lambda copy: copy.wait_send())


def local(
    sizes, states, anchor, step_index, sigmas, enc_w, noise_embed, qkv_w, out_w, up_w, down_w, dec_w
):
    _, lat_rows, width = states.shape
    channels, model = enc_w.shape
    columns = width // channels
    rows = lat_rows * width // LANES
    padded_rows = -(-rows // 16) * 16
    tokens = lat_rows * columns
    steps, bands = sizes
    f32, bf16 = jnp.float32, jnp.bfloat16
    weights = (enc_w, noise_embed, qkv_w, out_w, up_w, down_w, dec_w.T)
    hbm = pl.BlockSpec(memory_space=pl.ANY)
    smem = pl.BlockSpec(memory_space=pltpu.SMEM)
    dma = pltpu.SemaphoreType.DMA
    return pl.pallas_call(
        functools.partial(kernel, sizes),
        out_shape=(
            pltpu.VMEM(states.shape, f32),
            jax.ShapeDtypeStruct((1,), f32),
        ),
        in_specs=[smem, smem] + [hbm] * 9,
        out_specs=(pl.BlockSpec(memory_space=pltpu.VMEM), smem),
        scratch_shapes=[
            pltpu.VMEM((lat_rows, width), f32),
            pltpu.VMEM((lat_rows, width), f32),
        ]
        + [pltpu.VMEM(w.shape, w.dtype) for w in weights]
        + [
            pltpu.VMEM((rows, LANES), f32),
            pltpu.VMEM((rows, LANES), f32),
            pltpu.VMEM((padded_rows, LANES), bf16),
            pltpu.VMEM((3, padded_rows, LANES), bf16),
            pltpu.VMEM((3 * tokens, model), bf16),
            pltpu.VMEM((3 * tokens, 2 * model), bf16),
            pltpu.VMEM((tokens, model), bf16),
            pltpu.VMEM((tokens, LANES), f32),
            pltpu.VMEM((rows, LANES), f32),
            pltpu.VMEM((rows, LANES), f32),
            pltpu.VMEM((bands, 8, LANES), f32),
            dma((9,)),
            dma((5,)),
            dma((3,)),
            dma((CHUNKS,)),
            dma((CHUNKS,)),
            dma((bands - 1,)),
            dma((bands - 1,)),
        ],
        compiler_params=pltpu.CompilerParams(
            collective_id=0, has_side_effects=True, vmem_limit_bytes=(65536 - 512) * 1024
        ),
        cost_estimate=pl.CostEstimate(flops=2 * 10**9, bytes_accessed=5 * 10**6, transcendentals=10**6),
    )(step_index, sigmas, states, anchor, *weights)


def solution(mesh):
    placed = (
        P("step", "band", None), P("band", None), P("step"),
        P(), P(), P(), P(), P(), P(), P(), P(),
    )
    return jax.shard_map(
        functools.partial(local, (mesh.shape["step"], mesh.shape["band"])),
        mesh=mesh,
        in_specs=placed,
        out_specs=(P("step", "band", None), P("step")),
        check_vma=False,
    )
```
